512 devices in a mesh: dp: 4 (over y_hi), ctx: 16 (over z, y_lo), exp: 8 (over x, core).
Axes of the slice: x: 4, y: 8 (y_hi: 4, y_lo: 2; y = y_hi * 2 + y_lo), z: 8, core: 2. Of those that a mesh axis runs over, the one named last changes fastest.
Arguments:
- queries: bfloat16 [8192, 4096], P(('dp', 'ctx'), 'exp'), parts along dimension 0, may hold values from -200 to 200
- keys: bfloat16 [8192, 512], P(('dp', 'ctx')), parts along dimension 0, may hold values from -8 to 8
- values: bfloat16 [8192, 512], P(('dp', 'ctx')), parts along dimension 0, may hold values from -6 to 6
- resid: bfloat16 [8192, 2048], P(('dp', 'ctx', 'exp')), parts along dimension 0, may hold values from -3 to 3
- out_proj: bfloat16 [4096, 2048], P('exp'), may hold values from -0.09375 to 0.09375
- norm_gain: float32 [2048], replicated, may hold values from 0.1 to 1.9
- expert_ids: int32 [8192, 8], P(('dp', 'ctx', 'exp')), parts along dimension 0, may hold values from 0 to 15, all different within a row
- gate_probs: float32 [8192, 8], P(('dp', 'ctx', 'exp')), parts along dimension 0, may hold values from 0.02 to 0.4
- w_gate: bfloat16 [16, 2048, 384], P('exp', 'ctx'), may hold values from -0.125 to 0.125
- w_up: bfloat16 [16, 2048, 384], P('exp', 'ctx'), may hold values from -0.125 to 0.125
- w_down: bfloat16 [16, 384, 2048], P('exp', None, 'ctx'), may hold values from -0.3125 to 0.3125
Outputs:
- layer_out: bfloat16 [8192, 2048], P(('dp', 'ctx', 'exp')), parts along dimension 0
The draws below stay inside these ranges and needn't reach their ends.
There are 4 independent parts, one for each index of `dp`. The reference program is written for one: setup_inputs(seed, part) draws one part's arguments, and reference() takes and returns one part's arrays. A program takes and returns all parts, laid end to end along the dimension named above; an argument that names none is the same for every part. Nothing has to cross between parts.
Inputs may be any that keep to these rules, and one draw needn't show every extreme that they name: `expert_ids`: each row names 8 different experts.
All inputs are finite; a program needn't handle non-finite values.
Results may differ from the reference program's by a relative error of at most 0.018.
Values may be sent and summed in bfloat16 or wider, within the bound.
A program may use at most 64 MiB of HBM per device.

```python
import jax
import jax.numpy as jnp
from jax import lax

D = 2048
QH = 32
KVH = 4
HD = 128
FF = 384
EXPERTS = 16
TOPK = 8
LEN = 2048
ROWS_DEV = 16
CAP = 10
N_EXP = 8


def draw_queries(key, part):
    key = jax.random.fold_in(key, 11)
    own_key = jax.random.fold_in(key, 0)
    return jnp.clip(2.5 * jax.random.normal(own_key, (LEN, QH * HD), jnp.float32), -15.0, 15.0).astype(jnp.bfloat16)


def draw_keys(key, part):
    key = jax.random.fold_in(key, 12)
    own_key = jax.random.fold_in(key, 0)
    return jnp.clip(jax.random.normal(own_key, (LEN, KVH * HD), jnp.float32), -8.0, 8.0).astype(jnp.bfloat16)


def block_scale(key, dims, pieces, least, high):
    def one(position, shards_of):
        steps = jax.random.uniform(jax.random.fold_in(jax.random.fold_in(key, 6), position), (shards_of,), jnp.float32, least / len(pieces), high / len(pieces))
        return jnp.repeat(jnp.exp(steps), dims[position] // shards_of).reshape((-1,) + (1,) * (len(dims) - position - 1))

    loudness = one(*pieces[0])
    for cut in pieces[1:]:
        loudness = loudness * one(*cut)
    return loudness


def different_ones(key, rows, amount, top, lift):
    ranking = jax.random.permutation(jax.random.fold_in(key, 1), amount)
    pull = ranking
    for power in range(3):
        pull = pull * pull // amount
    pull = pull * lift // amount
    tickets = jax.random.randint(jax.random.fold_in(key, 2), (rows, amount), 0, 4096) + pull
    sure = jax.random.permutation(jax.random.fold_in(key, 3), rows)[jnp.arange(amount) % rows]
    tickets = jnp.where(jnp.arange(rows)[:, None] == sure[None, :], 1 << 14, tickets)
    score = tickets * amount + jnp.arange(amount)
    return lax.top_k(score.astype(jnp.int32), top)[1].astype(jnp.int32)


def normal_values(key, dims, scale, bound, cuts=(), kind=jnp.bfloat16):
    gain = block_scale(key, dims, cuts, -0.22, 0.18) if cuts else 1.0
    entries = jax.random.normal(key, dims, jnp.float32) * scale * gain
    return jnp.minimum(jnp.maximum(entries, -bound), bound).astype(kind)


def setup_inputs(seed: int = 0, part: int = 0) -> dict:
    key_of = jax.random.split(jax.random.key(seed), 12)
    part_splits = jax.random.split(jax.random.fold_in(key_of[11], part), 12)
    queries = draw_queries(jax.random.fold_in(jax.random.fold_in(key_of[11], part), 71), part)
    keys = draw_keys(jax.random.fold_in(jax.random.fold_in(key_of[11], part), 71), part)
    values = normal_values(part_splits[2], (LEN, KVH * HD), 1.0, 6.0, ((0, 16),))
    resid = normal_values(part_splits[3], (LEN, D), 0.5, 3.0, ((0, 128),))
    out_proj = normal_values(key_of[4], (QH * HD, D), (QH * HD) ** -0.5, 0.09375, ((0, 8),))
    norm_gain = jnp.clip(1.0 + 0.18 * jax.random.normal(key_of[5], (D,), jnp.float32), 0.1, 1.9)
    expert_ids = different_ones(part_splits[6], LEN, EXPERTS, TOPK, 8192)
    gate_probs = jnp.clip(0.02 + 0.38 * jax.random.uniform(part_splits[7], (LEN, TOPK), jnp.float32) ** block_scale(part_splits[7], (LEN, TOPK), ((0, 128),), -0.2, 0.2), 0.02, 0.4)
    w_gate = normal_values(key_of[8], (EXPERTS, D, FF), D ** -0.5, 0.125, ((0, 8), (1, 16)))
    w_up = normal_values(key_of[9], (EXPERTS, D, FF), D ** -0.5, 0.125, ((0, 8), (1, 16)))
    w_down = normal_values(key_of[10], (EXPERTS, FF, D), FF ** -0.5, 0.3125, ((0, 8), (2, 16)))
    return dict(queries=queries, keys=keys, values=values, resid=resid, out_proj=out_proj, norm_gain=norm_gain, expert_ids=expert_ids, gate_probs=gate_probs, w_gate=w_gate, w_up=w_up, w_down=w_down)


def reference(queries, keys, values, resid, out_proj, norm_gain, expert_ids, gate_probs, w_gate, w_up, w_down):
    head_group = QH // KVH
    scale = float(HD) ** (-0.5)
    positions = jnp.arange(LEN)
    causal = positions[None, :] <= positions[:, None]

    def one_head(head):
        kv_head = head // head_group
        query_cols = lax.dynamic_slice_in_dim(queries, (head * HD).astype(jnp.int32), HD, 1)
        key_cols = lax.dynamic_slice_in_dim(keys, (kv_head * HD).astype(jnp.int32), HD, 1)
        value_cols = lax.dynamic_slice_in_dim(values, (kv_head * HD).astype(jnp.int32), HD, 1)
        scores = jnp.dot(query_cols, key_cols.T, preferred_element_type=jnp.float32) * scale
        scores = jnp.where(causal, scores, -jnp.inf)
        peak = lax.optimization_barrier(jnp.max(scores, axis=1, keepdims=True))
        raw = jnp.where(causal, jnp.exp(scores - peak), 0.0)
        total = lax.optimization_barrier(jnp.sum(raw, axis=1, keepdims=True))
        mixed = jnp.dot(raw.astype(jnp.bfloat16), value_cols, preferred_element_type=jnp.float32)
        return (mixed / total).astype(jnp.bfloat16)
    per_head = lax.map(one_head, jnp.arange(QH, dtype=jnp.int32))
    attended = jnp.transpose(per_head, (1, 0, 2)).reshape(LEN, QH * HD)
    width = QH * HD // N_EXP
    projected = jnp.zeros((LEN, D), jnp.float32)
    for group_index in range(N_EXP):
        partial_term = jnp.dot(attended[:, group_index * width:(group_index + 1) * width], out_proj[group_index * width:(group_index + 1) * width, :], preferred_element_type=jnp.float32)
        projected = projected + partial_term.astype(jnp.bfloat16).astype(jnp.float32)
    mid = resid.astype(jnp.float32) + projected
    normed = (mid * lax.rsqrt(lax.optimization_barrier(jnp.mean(mid * mid, axis=1, keepdims=True)) + 1e-06) * norm_gain).astype(jnp.bfloat16)
    onehot = (expert_ids[:, :, None] == jnp.arange(EXPERTS, dtype=jnp.int32)[None, None, :]).astype(jnp.int32)
    blocked = onehot.reshape(LEN // ROWS_DEV, ROWS_DEV * TOPK, EXPERTS)
    earlier = jnp.cumsum(blocked, axis=1) - blocked
    rank = lax.optimization_barrier(jnp.sum(earlier * blocked, axis=2)).reshape(LEN, TOPK)
    kept = rank < CAP
    weights = jnp.where(kept, gate_probs, 0.0)

    def one_expert(total_out, expert):
        gate = jnp.dot(normed, w_gate[expert], preferred_element_type=jnp.float32)
        upper = jnp.dot(normed, w_up[expert], preferred_element_type=jnp.float32)
        hidden = (jax.nn.silu(gate) * upper).astype(jnp.bfloat16)
        result = jnp.dot(hidden, w_down[expert], preferred_element_type=jnp.float32).astype(jnp.bfloat16)
        coef = lax.optimization_barrier(jnp.sum(jnp.where(expert_ids == expert, weights, 0.0), axis=1))
        return (total_out + coef[:, None] * result.astype(jnp.float32), None)
    moe, _ = lax.scan(one_expert, jnp.zeros((LEN, D), jnp.float32), jnp.arange(EXPERTS, dtype=jnp.int32))
    return (mid + moe).astype(jnp.bfloat16)
```

```python
import functools

import jax
import jax.numpy as jnp
from jax import lax
from jax.experimental import pallas as pl
from jax.experimental.pallas import tpu as pltpu
from jax.sharding import PartitionSpec as P

MESH = pl.DeviceIdType.MESH
BF = jnp.bfloat16
F32 = jnp.float32
HD = 128
D = 2048
FF = 384
NZ = 8
NX = 4
CAP = 10
MSG = D + 128
N_SEM = 160


def layer_kernel(
    q_hbm,
    k_hbm,
    v_hbm,
    resid_hbm,
    op_hbm,
    gain_hbm,
    ids_hbm,
    probs_hbm,
    wg_hbm,
    wu_hbm,
    wd_hbm,
    out_ref,
    q4,
    kv,
    op,
    resid,
    gain,
    ids,
    probs,
    gate_w,
    up_w,
    down_w,
    m_run,
    l_run,
    acc,
    att,
    part,
    part_in,
    part_sum,
    head_in,
    mid_ref,
    rows,
    hid,
    moe,
    moe_in,
    moe_sum,
    moe_x,
    y_out,
    y_in,
    local_sem,
    send_sem,
    recv_sem,
):
    d = lax.axis_index("dp")
    i = lax.axis_index("ctx")
    e = lax.axis_index("exp")
    z, yl = lax.div(i, 2), lax.rem(i, 2)
    x, c = lax.div(e, 2), lax.rem(e, 2)
    role = lax.rem(d, 2)
    y = d * 2 + yl
    y_partner = lax.rem(y + 2 * yl - 1 + 8, 8)

    def zdev(dz):
        return (d, lax.rem(z + dz + NZ, NZ) * 2 + yl, e)

    def xdev(dx):
        return (d, i, lax.rem(x + dx, NX) * 2 + c)

    sibling = (d, i, x * 2 + 1 - c)
    pair = (d, z * 2 + 1 - yl, e)
    partner = (lax.div(y_partner, 2), z * 2 + lax.rem(y_partner, 2), e)

    keys = {}
    sent = []
    locals_ = {}

    def slot(key):
        return keys.setdefault(key, len(keys))

    def send(key, src, dst, device):
        n = slot(key)
        copy = pltpu.make_async_remote_copy(
            src_ref=src,
            dst_ref=dst,
            send_sem=send_sem.at[n],
            recv_sem=recv_sem.at[n],
            device_id=device,
            device_id_type=MESH,
        )
        copy.start()
        sent.append(copy)

    def arrive(key, dst):
        n = slot(key)
        pltpu.make_async_remote_copy(
            src_ref=dst,
            dst_ref=dst,
            send_sem=send_sem.at[n],
            recv_sem=recv_sem.at[n],
            device_id=sibling,
            device_id_type=MESH,
        ).wait_recv()

    def load(key, src, dst):
        copy = pltpu.make_async_copy(src, dst, local_sem.at[len(locals_)])
        copy.start()
        locals_[key] = copy

    def mod_z(dz):
        return lax.rem(z + dz + NZ, NZ)

    own_rows = pl.ds(pl.multiple_of(i * 128, 128), 128)
    head_cols = pl.ds(pl.multiple_of(x * HD, HD), HD)
    load("k", k_hbm.at[:, head_cols], kv.at[0, own_rows])
    load("v", v_hbm.at[:, head_cols], kv.at[1, own_rows])
    for h in range(4):
        load(("q", h), q_hbm.at[:, pl.ds(h * HD, HD)], q4.at[pl.ds(h * HD, HD)])
    load("op", op_hbm, op)
    load("resid", resid_hbm, resid)
    load("gain", gain_hbm, gain)
    load("ids", ids_hbm, ids)
    load("probs", probs_hbm, probs)

    def gate_at(s):
        return gate_w.at[pl.ds(pl.multiple_of(s * 128, 128), 128)]

    def up_at(s):
        return up_w.at[pl.ds(pl.multiple_of(s * 128, 128), 128)]

    def down_at(s):
        return down_w.at[:, pl.ds(pl.multiple_of(s * 128, 128), 128)]

    places = (gate_at, up_at, down_at)
    firsts = (wg_hbm.at[role], wu_hbm.at[role], wd_hbm.at[role])
    for p in range(3):
        load(("w", p), firsts[p], places[p](i))

    barrier = pltpu.get_barrier_semaphore()
    near = [zdev(1), zdev(-1), pair, partner, sibling, xdev(1), xdev(2), xdev(3)]
    for device in near:
        pl.semaphore_signal(barrier, inc=1, device_id=device, device_id_type=MESH)
    pl.semaphore_wait(barrier, len(near))

    def hops(p, w, direction):
        return 4 if ((p + w) % 2 == 0) == (direction > 0) else 3

    def shard(dz, w):
        return mod_z(dz) * 2 + (yl if w == 0 else 1 - yl)

    def weight_z(p, w, direction, hop):
        place = places[p](shard(-direction * hop, w))
        src = firsts[p] if (w == 0 and hop == 0) else place
        send(("wz", p, w, direction, hop), src, place, zdev(direction))

    def weight_y(p, dz):
        place = places[p](shard(dz, 0))
        src = firsts[p] if dz == 0 else place
        send(("wy", p, dz % NZ), src, place, pair)

    def weight_step(p, w, direction, hop):
        place = places[p](shard(-direction * (hop + 1), w))
        arrive(("wz", p, w, direction, hop), place)
        if hop + 1 < hops(p, w, direction):
            weight_z(p, w, direction, hop + 1)
        if p > 0:
            weight_y(p, -direction * (hop + 1))

    events = []
    for hop in range(4):
        for p, w in ((1, 0), (2, 0), (0, 0), (0, 1)):
            for direction in (1, -1):
                if hop < hops(p, w, direction):
                    events.append(functools.partial(weight_step, p, w, direction, hop))

    def pump(n):
        for _ in range(n):
            if events:
                events.pop(0)()

    def kv_at(kind, dz):
        return kv.at[kind, pl.ds(pl.multiple_of(mod_z(dz) * 256, 256), 256)]

    pair_rows = pl.ds(pl.multiple_of((z * 2 + 1 - yl) * 128, 128), 128)

    def kv_hops(direction):
        return 4 if direction > 0 else 3

    def kv_z(direction, hop):
        place = kv_at(c, -direction * hop)
        send(("kz", direction, hop), place, place, zdev(direction))

    locals_["k"].wait()
    locals_["v"].wait()
    send("kp", kv.at[c, own_rows], kv.at[c, own_rows], pair)
    weight_y(0, 0)
    for direction in (1, -1):
        weight_z(1, 0, direction, 0)

    arrive("kp", kv.at[c, pair_rows])
    for direction in (1, -1):
        kv_z(direction, 0)
    send("ks0", kv.at[c, pair_rows], kv.at[c, pair_rows], sibling)
    weight_y(1, 0)
    for direction in (1, -1):
        weight_z(2, 0, direction, 0)

    def block(dz, first):
        key_rows = pl.ds(pl.multiple_of(mod_z(dz) * 256, 256), 256)
        scores = lax.dot_general(
            kv[0, key_rows, :], q4[...], (((1,), (1,)), ((), ())), preferred_element_type=F32
        ) * (float(HD) ** -0.5)
        if first:
            key_pos = z * 256 + lax.broadcasted_iota(jnp.int32, (256, 512), 0)
            query_pos = i * 128 + lax.rem(lax.broadcasted_iota(jnp.int32, (256, 512), 1), 128)
            scores = jnp.where(key_pos <= query_pos, scores, -1e30)
        peak = jnp.max(scores, axis=0, keepdims=True)
        if not first:
            old = m_run[...]
            peak = jnp.maximum(peak, old)
        raw = jnp.exp(scores - peak)
        total = jnp.sum(raw, axis=0, keepdims=True)
        mixed = lax.dot_general(
            kv[1, key_rows, :],
            raw.astype(BF),
            (((0,), (0,)), ((), ())),
            preferred_element_type=F32,
        )
        m_run[...] = peak
        if first:
            l_run[...] = total
            acc[...] = mixed
        else:
            factor = jnp.exp(old - peak)
            l_run[...] = l_run[...] * factor + total
            acc[...] = acc[...] * factor + mixed

    for h in range(4):
        locals_[("q", h)].wait()
    arrive("ks0", kv.at[1 - c, pair_rows])
    block(0, True)

    for hop in range(4):
        around = [s for s in (1, -1) if hop < kv_hops(s)]
        for direction in around:
            place = kv_at(c, -direction * (hop + 1))
            arrive(("kz", direction, hop), place)
            if hop + 1 < kv_hops(direction):
                kv_z(direction, hop + 1)
            send(("ks", direction, hop), place, place, sibling)
        if hop == 0:
            weight_y(2, 0)
            for direction in (1, -1):
                weight_z(0, 0, direction, 0)
        if hop == 1:
            arrive(("wy", 0, 0), gate_at(z * 2 + 1 - yl))
            for direction in (1, -1):
                weight_z(0, 1, direction, 0)
        if hop == 2:
            pump(2)
        for direction in around:
            arrive(("ks", direction, hop), kv_at(1 - c, -direction * (hop + 1)))
        for direction in around:
            dz = -direction * (hop + 1)
            seen = (z + dz >= 0) if direction > 0 else (z + dz >= NZ)
            pl.when(seen)(functools.partial(block, dz, False))

    mixed = acc[...] / l_run[...]
    for h in range(4):
        att[:, h * HD : (h + 1) * HD] = mixed[:, h * HD : (h + 1) * HD].T.astype(BF)
    locals_["op"].wait()

    @pl.loop(0, 4)
    def _(n):
        cols = pl.ds(pl.multiple_of(n * 512, 512), 512)
        share = jnp.dot(att[...], op[:, cols], preferred_element_type=F32).astype(BF)
        for owner in range(8):
            part[owner % 2, owner // 2, :, cols] = share[owner * 16 : owner * 16 + 16]

    send("hs", part.at[1 - c], part_in, sibling)
    pump(2)

    for name in ("ids", "probs", "resid", "gain"):
        locals_[name].wait()
    lane = lax.broadcasted_iota(jnp.int32, (16, 128), 1)
    low = lax.rem(lane, 16)
    chosen = jnp.zeros((16, 128), F32)
    weight = jnp.zeros((16, 128), F32)
    for k in range(8):
        hit = ids[:, k : k + 1] == low
        chosen = jnp.where(hit, 1.0, chosen)
        weight = jnp.where(hit, probs[:, k : k + 1], weight)
    before = (
        lax.broadcasted_iota(jnp.int32, (16, 16), 1) < lax.broadcasted_iota(jnp.int32, (16, 16), 0)
    ).astype(BF)
    rank = jnp.dot(before, chosen.astype(BF), preferred_element_type=F32)
    weight = jnp.where(rank < CAP - 0.5, weight, 0.0)
    high = weight.astype(BF).astype(F32)
    middle = (weight - high).astype(BF).astype(F32)
    least = weight - high - middle
    coded = jnp.where(
        lane < 16, high, jnp.where(lane < 32, middle, jnp.where(lane < 48, least, 0.0))
    )
    rows[0, e, :, D:] = coded.astype(BF)

    arrive("hs", part_in)
    part_sum[...] = (part[c].astype(F32) + part_in[...].astype(F32)).astype(BF)
    for dx in (2, 1, 3):
        send(("hx", dx), part_sum.at[lax.rem(x + dx, NX)], head_in.at[dx - 1], xdev(dx))
    pump(8)
    mid = resid[...].astype(F32) + part_sum[x].astype(F32)
    for dx in (1, 3, 2):
        arrive(("hx", dx), head_in.at[dx - 1])
        mid = mid + head_in[dx - 1].astype(F32)
    mid_ref[...] = mid
    mean = jnp.mean(mid * mid, axis=1, keepdims=True)
    rows[0, e, :, :D] = (mid * lax.rsqrt(mean + 1e-06) * gain[...]).astype(BF)

    own = rows.at[0, e]
    send("ap", own, rows.at[1, e], partner)
    for dx in (2, 1, 3):
        send(("ax", 0, dx), own, own, xdev(dx))
    send(("as", 0, 0), own, own, sibling)
    pump(4)
    other = rows.at[1, e]
    arrive("ap", other)
    for dx in (2, 1, 3):
        send(("ax", 1, dx), other, other, xdev(dx))
    send(("as", 1, 0), other, other, sibling)
    for r in range(2):
        for dx in (1, 3, 2):
            come = rows.at[r, lax.rem(x - dx + NX, NX) * 2 + c]
            arrive(("ax", r, dx), come)
            send(("as", r, dx), come, come, sibling)
        pump(4)
    for r in range(2):
        for dx in range(4):
            arrive(("as", r, dx), rows.at[r, lax.rem(x - dx + NX, NX) * 2 + 1 - c])
    pump(100)
    for p in range(3):
        locals_[("w", p)].wait()

    tokens = rows[:, :, :, :D].reshape(256, D)
    gated = jnp.dot(tokens, gate_w[...], preferred_element_type=F32)
    for dz in range(NZ):
        arrive(("wy", 1, dz), up_at(shard(dz, 1)))
    upped = jnp.dot(tokens, up_w[...], preferred_element_type=F32)
    hid[...] = (gated / (1.0 + jnp.exp(-gated)) * upped).astype(BF)
    codes = rows[:, :, :, D:].reshape(256, 128).astype(F32)
    lanes = lax.broadcasted_iota(jnp.int32, (256, 128), 1)
    mine = (lax.rem(lanes, 16) == e * 2 + role) & (lanes < 48)
    coef = jnp.sum(jnp.where(mine, codes, 0.0), axis=1, keepdims=True)
    for dz in range(NZ):
        arrive(("wy", 2, dz), down_at(shard(dz, 1)))

    @pl.loop(0, 4)
    def _(n):
        cols = pl.ds(pl.multiple_of(n * 512, 512), 512)
        made = jnp.dot(hid[...], down_w[:, cols], preferred_element_type=F32)
        made = (made.astype(BF).astype(F32) * coef).astype(BF)
        for r in range(2):
            for owner in range(8):
                first = r * 128 + owner * 16
                moe[owner % 2, r, owner // 2, :, cols] = made[first : first + 16]

    send("ms", moe.at[1 - c], moe_in, sibling)
    arrive("ms", moe_in)
    for r in (1, 0):
        moe_sum[r] = (moe[c, r].astype(F32) + moe_in[r].astype(F32)).astype(BF)
        for dx in (2, 1, 3):
            send(
                ("mx", r, dx), moe_sum.at[r, lax.rem(x + dx, NX)], moe_x.at[r, dx - 1], xdev(dx)
            )
    total = moe_sum[1, x].astype(F32)
    for dx in (1, 3, 2):
        arrive(("mx", 1, dx), moe_x.at[1, dx - 1])
        total = total + moe_x[1, dx - 1].astype(F32)
    y_out[...] = total.astype(BF)
    send("my", y_out, y_in, partner)
    total = mid_ref[...] + moe_sum[0, x].astype(F32)
    for dx in (1, 3, 2):
        arrive(("mx", 0, dx), moe_x.at[0, dx - 1])
        total = total + moe_x[0, dx - 1].astype(F32)
    for copy in sent:
        copy.wait_send()
    arrive("my", y_in)
    out_ref[...] = (total + y_in[...].astype(F32)).astype(BF)
    assert len(keys) <= N_SEM


def on_device(
    queries, keys, values, resid, out_proj, norm_gain, expert_ids, gate_probs, w_gate, w_up, w_down
):
    anywhere = pl.BlockSpec(memory_space=pl.ANY)
    return pl.pallas_call(
        layer_kernel,
        out_shape=jax.ShapeDtypeStruct((16, D), BF),
        in_specs=[anywhere] * 11,
        out_specs=pl.BlockSpec(memory_space=pltpu.VMEM),
        scratch_shapes=[
            pltpu.VMEM((512, HD), BF),
            pltpu.VMEM((2, 2048, HD), BF),
            pltpu.VMEM((512, D), BF),
            pltpu.VMEM((16, D), BF),
            pltpu.VMEM((1, D), F32),
            pltpu.VMEM((16, 8), jnp.int32),
            pltpu.VMEM((16, 8), F32),
            pltpu.VMEM((D, FF), BF),
            pltpu.VMEM((D, FF), BF),
            pltpu.VMEM((FF, D), BF),
            pltpu.VMEM((1, 512), F32),
            pltpu.VMEM((1, 512), F32),
            pltpu.VMEM((HD, 512), F32),
            pltpu.VMEM((128, 512), BF),
            pltpu.VMEM((2, 4, 16, D), BF),
            pltpu.VMEM((4, 16, D), BF),
            pltpu.VMEM((4, 16, D), BF),
            pltpu.VMEM((3, 16, D), BF),
            pltpu.VMEM((16, D), F32),
            pltpu.VMEM((2, 8, 16, MSG), BF),
            pltpu.VMEM((256, FF), BF),
            pltpu.VMEM((2, 2, 4, 16, D), BF),
            pltpu.VMEM((2, 4, 16, D), BF),
            pltpu.VMEM((2, 4, 16, D), BF),
            pltpu.VMEM((2, 3, 16, D), BF),
            pltpu.VMEM((16, D), BF),
            pltpu.VMEM((16, D), BF),
            pltpu.SemaphoreType.DMA((16,)),
            pltpu.SemaphoreType.DMA((N_SEM,)),
            pltpu.SemaphoreType.DMA((N_SEM,)),
        ],
        compiler_params=pltpu.CompilerParams(
            collective_id=0, has_side_effects=True, vmem_limit_bytes=40 << 20
        ),
        cost_estimate=pl.CostEstimate(
            flops=2_000_000_000, bytes_accessed=6_000_000, transcendentals=1_000_000
        ),
        name="layer",
    )(
        queries,
        keys,
        values,
        resid,
        out_proj,
        norm_gain.reshape(1, D),
        expert_ids,
        gate_probs,
        w_gate,
        w_up,
        w_down,
    )


def solution(mesh):
    placed = (
        P(("dp", "ctx"), "exp"),
        P(("dp", "ctx"), None),
        P(("dp", "ctx"), None),
        P(("dp", "ctx", "exp"), None),
        P("exp", None),
        P(),
        P(("dp", "ctx", "exp"), None),
        P(("dp", "ctx", "exp"), None),
        P("exp", "ctx", None),
        P("exp", "ctx", None),
        P("exp", None, "ctx"),
    )
    return jax.shard_map(
        on_device,
        mesh=mesh,
        in_specs=placed,
        out_specs=P(("dp", "ctx", "exp"), None),
        check_vma=False,
    )
```

```python
import functools

import jax
import jax.numpy as jnp
from jax import lax
from jax.experimental import pallas as pl
from jax.experimental.pallas import tpu as pltpu
from jax.sharding import PartitionSpec as P

MESH = pl.DeviceIdType.MESH
BF = jnp.bfloat16
F32 = jnp.float32
HD = 128
D = 2048
FF = 384
NZ = 8
NX = 4
CAP = 10
MSG = D + 128
N_SEM = 160
STEPS = (2, 1, 1, 1, 1, 1, 1, 1, 1, 1, 1, 1, 1, 2, 2, 2, 1)


def layer_kernel(
    q_hbm,
    k_hbm,
    v_hbm,
    resid_hbm,
    op_hbm,
    gain_hbm,
    ids_hbm,
    probs_hbm,
    wg_hbm,
    wu_hbm,
    wd_hbm,
    out_ref,
    q4,
    kv,
    op,
    resid,
    gain,
    ids,
    probs,
    turn,
    gate_w,
    up_w,
    down_w,
    m_run,
    l_run,
    acc,
    att,
    part,
    part_in,
    part_sum,
    head_in,
    mid_ref,
    rows,
    hid,
    moe,
    moe_in,
    moe_sum,
    moe_x,
    y_out,
    y_in,
    local_sem,
    send_sem,
    recv_sem,
):
    d = lax.axis_index("dp")
    i = lax.axis_index("ctx")
    e = lax.axis_index("exp")
    z, yl = lax.div(i, 2), lax.rem(i, 2)
    x, c = lax.div(e, 2), lax.rem(e, 2)
    role = lax.rem(d, 2)
    y = d * 2 + yl
    y_partner = lax.rem(y + 2 * yl - 1 + 8, 8)

    def zdev(dz):
        return (d, lax.rem(z + dz + NZ, NZ) * 2 + yl, e)

    def xdev(dx):
        return (d, i, lax.rem(x + dx, NX) * 2 + c)

    sibling = (d, i, x * 2 + 1 - c)
    pair = (d, z * 2 + 1 - yl, e)
    partner = (lax.div(y_partner, 2), z * 2 + lax.rem(y_partner, 2), e)

    keys = {}
    sent = []
    locals_ = {}

    def slot(key):
        return keys.setdefault(key, len(keys))

    def send(key, src, dst, device):
        n = slot(key)
        copy = pltpu.make_async_remote_copy(
            src_ref=src,
            dst_ref=dst,
            send_sem=send_sem.at[n],
            recv_sem=recv_sem.at[n],
            device_id=device,
            device_id_type=MESH,
        )
        copy.start()
        sent.append(copy)

    def arrive(key, dst):
        n = slot(key)
        pltpu.make_async_remote_copy(
            src_ref=dst,
            dst_ref=dst,
            send_sem=send_sem.at[n],
            recv_sem=recv_sem.at[n],
            device_id=sibling,
            device_id_type=MESH,
        ).wait_recv()

    def load(key, src, dst):
        copy = pltpu.make_async_copy(src, dst, local_sem.at[len(locals_)])
        copy.start()
        locals_[key] = copy

    def mod_z(dz):
        return lax.rem(z + dz + NZ, NZ)

    own_rows = pl.ds(pl.multiple_of(i * 128, 128), 128)
    head_cols = pl.ds(pl.multiple_of(x * HD, HD), HD)
    load("k", k_hbm.at[:, head_cols], kv.at[0, own_rows])
    load("v", v_hbm.at[:, head_cols], kv.at[1, own_rows])
    for h in range(4):
        load(("q", h), q_hbm.at[:, pl.ds(h * HD, HD)], q4.at[pl.ds(h * HD, HD)])
    load("op", op_hbm, op)
    load("resid", resid_hbm, resid)
    load("gain", gain_hbm, gain)
    load("ids", ids_hbm, ids)
    load("probs", probs_hbm, probs)

    def gate_at(s):
        return gate_w.at[pl.ds(pl.multiple_of(s * 128, 128), 128)]

    def up_at(s):
        return up_w.at[pl.ds(pl.multiple_of(s * 128, 128), 128)]

    def down_at(s):
        return down_w.at[:, pl.ds(pl.multiple_of(s * 128, 128), 128)]

    places = (gate_at, up_at, down_at)
    firsts = (wg_hbm.at[role], wu_hbm.at[role], wd_hbm.at[role])
    for p in range(3):
        load(("w", p), firsts[p], places[p](i))

    barrier = pltpu.get_barrier_semaphore()
    near = [zdev(1), zdev(-1), pair, partner, sibling, xdev(1), xdev(2), xdev(3)]
    for device in near:
        pl.semaphore_signal(barrier, inc=1, device_id=device, device_id_type=MESH)
    pl.semaphore_wait(barrier, len(near))

    def hops(p, w, direction):
        return 4 if ((p + w) % 2 == 0) == (direction > 0) else 3

    def shard(dz, w):
        return mod_z(dz) * 2 + (yl if w == 0 else 1 - yl)

    def weight_z(p, w, direction, hop):
        place = places[p](shard(-direction * hop, w))
        src = firsts[p] if (w == 0 and hop == 0) else place
        send(("wz", p, w, direction, hop), src, place, zdev(direction))

    def weight_y(p, dz):
        place = places[p](shard(dz, 0))
        src = firsts[p] if dz == 0 else place
        send(("wy", p, dz % NZ), src, place, pair)

    def weight_step(p, w, direction, hop):
        place = places[p](shard(-direction * (hop + 1), w))
        arrive(("wz", p, w, direction, hop), place)
        if hop + 1 < hops(p, w, direction):
            weight_z(p, w, direction, hop + 1)
        if p > 0:
            weight_y(p, -direction * (hop + 1))

    def weight_start(p, w):
        if w == 1:
            arrive(("wy", p, 0), places[p](shard(0, 1)))
        for direction in (1, -1):
            weight_z(p, w, direction, 0)

    def weight_hop(p, w, hop):
        for direction in (1, -1):
            if hop < hops(p, w, direction):
                weight_step(p, w, direction, hop)

    streams = ((1, 0), (2, 0), (0, 0), (0, 1))
    events = [functools.partial(weight_start, p, w) for p, w in streams]
    for hop in range(4):
        events += [functools.partial(weight_hop, p, w, hop) for p, w in streams]
    points = list(STEPS)

    def point():
        for _ in range(points.pop(0) if points else len(events)):
            if events:
                events.pop(0)()

    def kv_at(kind, dz):
        return kv.at[kind, pl.ds(pl.multiple_of(mod_z(dz) * 256, 256), 256)]

    pair_rows = pl.ds(pl.multiple_of((z * 2 + 1 - yl) * 128, 128), 128)

    def kv_hops(direction):
        return 4 if direction > 0 else 3

    def kv_z(direction, hop):
        place = kv_at(c, -direction * hop)
        send(("kz", direction, hop), place, place, zdev(direction))

    locals_["k"].wait()
    locals_["v"].wait()
    send("kp", kv.at[c, own_rows], kv.at[c, own_rows], pair)
    for p in range(3):
        weight_y(p, 0)
    point()

    arrive("kp", kv.at[c, pair_rows])
    for direction in (1, -1):
        kv_z(direction, 0)
    send("ks0", kv.at[c, pair_rows], kv.at[c, pair_rows], sibling)
    point()

    def block(dz, first):
        key_rows = pl.ds(pl.multiple_of(mod_z(dz) * 256, 256), 256)
        scores = lax.dot_general(
            kv[0, key_rows, :], q4[...], (((1,), (1,)), ((), ())), preferred_element_type=F32
        ) * (float(HD) ** -0.5)
        if first:
            key_pos = z * 256 + lax.broadcasted_iota(jnp.int32, (256, 512), 0)
            query_pos = i * 128 + lax.rem(lax.broadcasted_iota(jnp.int32, (256, 512), 1), 128)
            scores = jnp.where(key_pos <= query_pos, scores, -1e30)
        peak = jnp.max(scores, axis=0, keepdims=True)
        if not first:
            old = m_run[...]
            peak = jnp.maximum(peak, old)
        raw = jnp.exp(scores - peak)
        total = jnp.sum(raw, axis=0, keepdims=True)
        mixed = lax.dot_general(
            kv[1, key_rows, :],
            raw.astype(BF),
            (((0,), (0,)), ((), ())),
            preferred_element_type=F32,
        )
        m_run[...] = peak
        if first:
            l_run[...] = total
            acc[...] = mixed
        else:
            factor = jnp.exp(old - peak)
            l_run[...] = l_run[...] * factor + total
            acc[...] = acc[...] * factor + mixed

    for h in range(4):
        locals_[("q", h)].wait()
    arrive("ks0", kv.at[1 - c, pair_rows])
    block(0, True)

    for hop in range(4):
        around = [s for s in (1, -1) if hop < kv_hops(s)]
        for direction in around:
            place = kv_at(c, -direction * (hop + 1))
            arrive(("kz", direction, hop), place)
            if hop + 1 < kv_hops(direction):
                kv_z(direction, hop + 1)
            send(("ks", direction, hop), place, place, sibling)
        point()
        for direction in around:
            arrive(("ks", direction, hop), kv_at(1 - c, -direction * (hop + 1)))
        for direction in around:
            dz = -direction * (hop + 1)
            seen = (z + dz >= 0) if direction > 0 else (z + dz >= NZ)
            pl.when(seen)(functools.partial(block, dz, False))
        point()

    mixed = acc[...] / l_run[...]
    for h in range(4):
        att[:, h * HD : (h + 1) * HD] = mixed[:, h * HD : (h + 1) * HD].T.astype(BF)
    locals_["op"].wait()

    @pl.loop(0, 4)
    def _(n):
        cols = pl.ds(pl.multiple_of(n * 512, 512), 512)
        share = jnp.dot(att[...], op[:, cols], preferred_element_type=F32).astype(BF)
        for owner in range(8):
            part[owner % 2, owner // 2, :, cols] = share[owner * 16 : owner * 16 + 16]

    send("hs", part.at[1 - c], part_in, sibling)
    point()

    for name in ("ids", "probs", "resid", "gain"):
        locals_[name].wait()
    turn[...] = jnp.zeros_like(turn)
    turn[0, :8, :16] = ids[...].astype(F32)
    turn[1, :8, :16] = probs[...]
    ids_of = turn[0].T
    probs_of = turn[1].T
    lane = lax.broadcasted_iota(jnp.int32, (16, 128), 1)
    low = lax.rem(lane, 16).astype(F32)
    chosen = jnp.zeros((16, 128), F32)
    weight = jnp.zeros((16, 128), F32)
    for k in range(8):
        hit = ids_of[:16, k : k + 1] == low
        chosen = jnp.where(hit, 1.0, chosen)
        weight = jnp.where(hit, probs_of[:16, k : k + 1], weight)
    before = (
        lax.broadcasted_iota(jnp.int32, (16, 16), 1) < lax.broadcasted_iota(jnp.int32, (16, 16), 0)
    ).astype(BF)
    rank = jnp.dot(before, chosen.astype(BF), preferred_element_type=F32)
    weight = jnp.where(rank < CAP - 0.5, weight, 0.0)
    high = weight.astype(BF).astype(F32)
    middle = (weight - high).astype(BF).astype(F32)
    least = weight - high - middle
    coded = jnp.where(
        lane < 16, high, jnp.where(lane < 32, middle, jnp.where(lane < 48, least, 0.0))
    )
    rows[0, e, :, D:] = coded.astype(BF)

    arrive("hs", part_in)
    part_sum[...] = (part[c].astype(F32) + part_in[...].astype(F32)).astype(BF)
    for dx in (2, 1, 3):
        send(("hx", dx), part_sum.at[lax.rem(x + dx, NX)], head_in.at[dx - 1], xdev(dx))
    point()
    mid = resid[...].astype(F32) + part_sum[x].astype(F32)
    for dx in (1, 3, 2):
        if dx == 2:
            point()
        arrive(("hx", dx), head_in.at[dx - 1])
        mid = mid + head_in[dx - 1].astype(F32)
    mid_ref[...] = mid
    mean = jnp.mean(mid * mid, axis=1, keepdims=True)
    rows[0, e, :, :D] = (mid * lax.rsqrt(mean + 1e-06) * gain[...]).astype(BF)

    own = rows.at[0, e]
    send("ap", own, rows.at[1, e], partner)
    for dx in (2, 1, 3):
        send(("ax", 0, dx), own, own, xdev(dx))
    send(("as", 0, 0), own, own, sibling)
    point()
    other = rows.at[1, e]
    arrive("ap", other)
    for dx in (2, 1, 3):
        send(("ax", 1, dx), other, other, xdev(dx))
    send(("as", 1, 0), other, other, sibling)
    point()
    for r in range(2):
        for dx in (1, 3, 2):
            come = rows.at[r, lax.rem(x - dx + NX, NX) * 2 + c]
            arrive(("ax", r, dx), come)
            send(("as", r, dx), come, come, sibling)
        point()
    for r in range(2):
        for dx in range(4):
            arrive(("as", r, dx), rows.at[r, lax.rem(x - dx + NX, NX) * 2 + 1 - c])
    point()
    for p in range(3):
        locals_[("w", p)].wait()

    tokens = rows[:, :, :, :D].reshape(256, D)
    gated = jnp.dot(tokens, gate_w[...], preferred_element_type=F32)
    for dz in range(NZ):
        arrive(("wy", 1, dz), up_at(shard(dz, 1)))
    upped = jnp.dot(tokens, up_w[...], preferred_element_type=F32)
    hid[...] = (gated / (1.0 + jnp.exp(-gated)) * upped).astype(BF)
    codes = rows[:, :, :, D:].reshape(256, 128).astype(F32)
    lanes = lax.broadcasted_iota(jnp.int32, (256, 128), 1)
    mine = (lax.rem(lanes, 16) == e * 2 + role) & (lanes < 48)
    coef = jnp.sum(jnp.where(mine, codes, 0.0), axis=1, keepdims=True)
    for dz in range(NZ):
        arrive(("wy", 2, dz), down_at(shard(dz, 1)))

    for r in (1, 0):

        @pl.loop(0, 4)
        def _(n):
            cols = pl.ds(pl.multiple_of(n * 512, 512), 512)
            own_hid = hid[r * 128 : r * 128 + 128]
            made = jnp.dot(own_hid, down_w[:, cols], preferred_element_type=F32)
            made = (made.astype(BF).astype(F32) * coef[r * 128 : r * 128 + 128]).astype(BF)
            for owner in range(8):
                moe[owner % 2, r, owner // 2, :, cols] = made[owner * 16 : owner * 16 + 16]

        send(("ms", r), moe.at[1 - c, r], moe_in.at[r], sibling)
    for r in (1, 0):
        arrive(("ms", r), moe_in.at[r])
        moe_sum[r] = (moe[c, r].astype(F32) + moe_in[r].astype(F32)).astype(BF)
        for dx in (2, 1, 3):
            send(
                ("mx", r, dx), moe_sum.at[r, lax.rem(x + dx, NX)], moe_x.at[r, dx - 1], xdev(dx)
            )
    total = moe_sum[1, x].astype(F32)
    for dx in (1, 3, 2):
        arrive(("mx", 1, dx), moe_x.at[1, dx - 1])
        total = total + moe_x[1, dx - 1].astype(F32)
    y_out[...] = total.astype(BF)
    send("my", y_out, y_in, partner)
    total = mid_ref[...] + moe_sum[0, x].astype(F32)
    for dx in (1, 3, 2):
        arrive(("mx", 0, dx), moe_x.at[0, dx - 1])
        total = total + moe_x[0, dx - 1].astype(F32)
    for copy in sent:
        copy.wait_send()
    arrive("my", y_in)
    out_ref[...] = (total + y_in[...].astype(F32)).astype(BF)
    assert len(keys) <= N_SEM


def on_device(
    queries, keys, values, resid, out_proj, norm_gain, expert_ids, gate_probs, w_gate, w_up, w_down
):
    in_hbm = pl.BlockSpec(memory_space=pltpu.HBM)
    return pl.pallas_call(
        layer_kernel,
        out_shape=jax.ShapeDtypeStruct((16, D), BF),
        in_specs=[in_hbm] * 11,
        out_specs=pl.BlockSpec(memory_space=pltpu.VMEM),
        scratch_shapes=[
            pltpu.VMEM((512, HD), BF),
            pltpu.VMEM((2, 2048, HD), BF),
            pltpu.VMEM((512, D), BF),
            pltpu.VMEM((16, D), BF),
            pltpu.VMEM((1, D), F32),
            pltpu.VMEM((8, 16), jnp.int32),
            pltpu.VMEM((8, 16), F32),
            pltpu.VMEM((2, 128, 128), F32),
            pltpu.VMEM((D, FF), BF),
            pltpu.VMEM((D, FF), BF),
            pltpu.VMEM((FF, D), BF),
            pltpu.VMEM((1, 512), F32),
            pltpu.VMEM((1, 512), F32),
            pltpu.VMEM((HD, 512), F32),
            pltpu.VMEM((128, 512), BF),
            pltpu.VMEM((2, 4, 16, D), BF),
            pltpu.VMEM((4, 16, D), BF),
            pltpu.VMEM((4, 16, D), BF),
            pltpu.VMEM((3, 16, D), BF),
            pltpu.VMEM((16, D), F32),
            pltpu.VMEM((2, 8, 16, MSG), BF),
            pltpu.VMEM((256, FF), BF),
            pltpu.VMEM((2, 2, 4, 16, D), BF),
            pltpu.VMEM((2, 4, 16, D), BF),
            pltpu.VMEM((2, 4, 16, D), BF),
            pltpu.VMEM((2, 3, 16, D), BF),
            pltpu.VMEM((16, D), BF),
            pltpu.VMEM((16, D), BF),
            pltpu.SemaphoreType.DMA((16,)),
            pltpu.SemaphoreType.DMA((N_SEM,)),
            pltpu.SemaphoreType.DMA((N_SEM,)),
        ],
        compiler_params=pltpu.CompilerParams(
            collective_id=0, has_side_effects=True, vmem_limit_bytes=58 << 20
        ),
        cost_estimate=pl.CostEstimate(
            flops=2_000_000_000, bytes_accessed=6_000_000, transcendentals=1_000_000
        ),
        name="layer",
    )(
        queries,
        keys,
        values,
        resid,
        out_proj,
        norm_gain.reshape(1, D),
        expert_ids.T,
        gate_probs.T,
        w_gate,
        w_up,
        w_down,
    )


def solution(mesh):
    placed = (
        P(("dp", "ctx"), "exp"),
        P(("dp", "ctx"), None),
        P(("dp", "ctx"), None),
        P(("dp", "ctx", "exp"), None),
        P("exp", None),
        P(),
        P(("dp", "ctx", "exp"), None),
        P(("dp", "ctx", "exp"), None),
        P("exp", "ctx", None),
        P("exp", "ctx", None),
        P("exp", None, "ctx"),
    )
    return jax.shard_map(
        on_device,
        mesh=mesh,
        in_specs=placed,
        out_specs=P(("dp", "ctx", "exp"), None),
        check_vma=False,
    )
```

```python
import functools

import jax
import jax.numpy as jnp
from jax import lax
from jax.experimental import pallas as pl
from jax.experimental.pallas import tpu as pltpu
from jax.sharding import PartitionSpec as P

MESH = pl.DeviceIdType.MESH
BF = jnp.bfloat16
F32 = jnp.float32
HD = 128
D = 2048
FF = 384
NZ = 8
NX = 4
CAP = 10
MSG = D + 128
N_SEM = 160
STEPS = (2, 1, 1, 1, 1, 1, 1, 1, 1, 1, 1, 2, 0, 2, 2, 2, 1)


def layer_kernel(
    q_hbm,
    k_hbm,
    v_hbm,
    resid_hbm,
    op_hbm,
    gain_hbm,
    ids_hbm,
    probs_hbm,
    wg_hbm,
    wu_hbm,
    wd_hbm,
    out_ref,
    q4,
    kv,
    op,
    resid,
    gain,
    ids,
    probs,
    turn,
    gate_w,
    up_w,
    down_w,
    m_run,
    l_run,
    acc,
    att,
    part,
    part_in,
    part_sum,
    head_in,
    mid_ref,
    rows,
    hid,
    upped,
    moe,
    moe_in,
    moe_sum,
    moe_x,
    y_out,
    y_in,
    local_sem,
    send_sem,
    recv_sem,
):
    d = lax.axis_index("dp")
    i = lax.axis_index("ctx")
    e = lax.axis_index("exp")
    z, yl = lax.div(i, 2), lax.rem(i, 2)
    x, c = lax.div(e, 2), lax.rem(e, 2)
    role = lax.rem(d, 2)
    y = d * 2 + yl
    y_partner = lax.rem(y + 2 * yl - 1 + 8, 8)

    def zdev(dz):
        return (d, lax.rem(z + dz + NZ, NZ) * 2 + yl, e)

    def xdev(dx):
        return (d, i, lax.rem(x + dx, NX) * 2 + c)

    sibling = (d, i, x * 2 + 1 - c)
    pair = (d, z * 2 + 1 - yl, e)
    partner = (lax.div(y_partner, 2), z * 2 + lax.rem(y_partner, 2), e)

    keys = {}
    sent = []
    sent_if = []
    locals_ = {}

    def slot(key):
        return keys.setdefault(key, len(keys))

    def send(key, src, dst, device, cond=None):
        n = slot(key)
        copy = pltpu.make_async_remote_copy(
            src_ref=src,
            dst_ref=dst,
            send_sem=send_sem.at[n],
            recv_sem=recv_sem.at[n],
            device_id=device,
            device_id_type=MESH,
        )
        copy.start()
        if cond is None:
            sent.append(copy)
        else:
            sent_if.append((cond, n, src.shape[0]))

    def arrive(key, dst):
        n = slot(key)
        pltpu.make_async_remote_copy(
            src_ref=dst,
            dst_ref=dst,
            send_sem=send_sem.at[n],
            recv_sem=recv_sem.at[n],
            device_id=sibling,
            device_id_type=MESH,
        ).wait_recv()

    def load(key, src, dst):
        copy = pltpu.make_async_copy(src, dst, local_sem.at[len(locals_)])
        copy.start()
        locals_[key] = copy

    def mod_z(dz):
        return lax.rem(z + dz + NZ, NZ)

    own_rows = pl.ds(pl.multiple_of(i * 128, 128), 128)
    head_cols = pl.ds(pl.multiple_of(x * HD, HD), HD)
    load("k", k_hbm.at[:, head_cols], kv.at[0, own_rows])
    load("v", v_hbm.at[:, head_cols], kv.at[1, own_rows])
    for h in range(4):
        load(("q", h), q_hbm.at[:, pl.ds(h * HD, HD)], q4.at[pl.ds(h * HD, HD)])
    load("op", op_hbm, op)
    load("resid", resid_hbm, resid)
    load("gain", gain_hbm, gain)
    load("ids", ids_hbm, ids)
    load("probs", probs_hbm, probs)

    def gate_at(s):
        return gate_w.at[pl.ds(pl.multiple_of(s * 128, 128), 128)]

    def up_at(s):
        return up_w.at[pl.ds(pl.multiple_of(s * 128, 128), 128)]

    def down_at(s):
        return down_w.at[:, pl.ds(pl.multiple_of(s * 128, 128), 128)]

    places = (gate_at, up_at, down_at)
    firsts = (wg_hbm.at[role], wu_hbm.at[role], wd_hbm.at[role])
    others = (wg_hbm.at[1 - role], wu_hbm.at[1 - role], wd_hbm.at[1 - role])
    for p in range(3):
        load(("w", p), firsts[p], places[p](i))

    barrier = pltpu.get_barrier_semaphore()
    near = [zdev(1), zdev(-1), pair, partner, sibling, xdev(1), xdev(2), xdev(3)]
    for device in near:
        pl.semaphore_signal(barrier, inc=1, device_id=device, device_id_type=MESH)
    pl.semaphore_wait(barrier, len(near))

    def hops(p, w, direction):
        return 4 if ((p + w) % 2 == 0) == (direction > 0) else 3

    def shard(dz, w):
        return mod_z(dz) * 2 + (yl if w == 0 else 1 - yl)

    def weight_z(p, w, direction, hop):
        place = places[p](shard(-direction * hop, w))
        src = firsts[p] if (w == 0 and hop == 0) else place
        send(("wz", p, w, direction, hop), src, place, zdev(direction))

    def weight_y(p, dz):
        place = places[p](shard(dz, 0))
        if dz == 0:
            send(("wy", p, 0), others[p], place, partner)
        else:
            send(("wy", p, dz % NZ), place, place, pair)

    def weight_step(p, w, direction, hop):
        place = places[p](shard(-direction * (hop + 1), w))
        arrive(("wz", p, w, direction, hop), place)
        if hop + 1 < hops(p, w, direction):
            weight_z(p, w, direction, hop + 1)
        if p > 0:
            weight_y(p, -direction * (hop + 1))

    def weight_start(p, w):
        if w == 1:
            arrive(("wy", p, 0), places[p](shard(0, 1)))
        for direction in (1, -1):
            weight_z(p, w, direction, 0)

    def weight_hop(p, w, hop):
        for direction in (1, -1):
            if hop < hops(p, w, direction):
                weight_step(p, w, direction, hop)

    streams = ((1, 0), (2, 0), (0, 0), (0, 1))
    events = [functools.partial(weight_start, p, w) for p, w in streams]
    for hop in range(4):
        events += [functools.partial(weight_hop, p, w, hop) for p, w in streams]
    points = list(STEPS)

    def point():
        for _ in range(points.pop(0) if points else len(events)):
            if events:
                events.pop(0)()

    def kv_at(kind, dz):
        return kv.at[kind, pl.ds(pl.multiple_of(mod_z(dz) * 256, 256), 256)]

    pair_rows = pl.ds(pl.multiple_of((z * 2 + 1 - yl) * 128, 128), 128)

    def kv_got(direction, hop):
        if direction > 0:
            return z >= hop + 1
        return ((z == 7) | (z <= 1), (z >= 6) | (z == 0), z >= 5)[hop]

    def kv_used(direction, hop):
        return z >= hop + 1 if direction > 0 else z + hop + 1 >= NZ

    def kv_more(direction, hop):
        if hop == 0:
            return z <= NZ - 2 if direction > 0 else z <= 2
        got = kv_got(direction, hop - 1)
        return got & (z <= NZ - 2) if direction > 0 else got

    def kv_z(direction, hop):
        more = kv_more(direction, hop)

        @pl.when(more)
        def _():
            place = kv_at(c, -direction * hop)
            send(("kz", direction, hop), place, place, zdev(direction), more)

    locals_["k"].wait()
    locals_["v"].wait()
    send("kp", kv.at[c, own_rows], kv.at[c, own_rows], pair)
    for p in range(3):
        weight_y(p, 0)
    point()

    arrive("kp", kv.at[c, pair_rows])
    for direction in (1, -1):
        kv_z(direction, 0)
    send("ks0", kv.at[c, pair_rows], kv.at[c, pair_rows], sibling)
    point()

    def block(dz, first):
        key_rows = pl.ds(pl.multiple_of(mod_z(dz) * 256, 256), 256)
        scores = lax.dot_general(
            kv[0, key_rows, :], q4[...], (((1,), (1,)), ((), ())), preferred_element_type=F32
        ) * (float(HD) ** -0.5)
        if first:
            key_pos = z * 256 + lax.broadcasted_iota(jnp.int32, (256, 512), 0)
            query_pos = i * 128 + lax.rem(lax.broadcasted_iota(jnp.int32, (256, 512), 1), 128)
            scores = jnp.where(key_pos <= query_pos, scores, -1e30)
        peak = jnp.max(scores, axis=0, keepdims=True)
        if not first:
            old = m_run[...]
            peak = jnp.maximum(peak, old)
        raw = jnp.exp(scores - peak)
        total = jnp.sum(raw, axis=0, keepdims=True)
        mixed = lax.dot_general(
            kv[1, key_rows, :],
            raw.astype(BF),
            (((0,), (0,)), ((), ())),
            preferred_element_type=F32,
        )
        m_run[...] = peak
        if first:
            l_run[...] = total
            acc[...] = mixed
        else:
            factor = jnp.exp(old - peak)
            l_run[...] = l_run[...] * factor + total
            acc[...] = acc[...] * factor + mixed

    for h in range(4):
        locals_[("q", h)].wait()
    arrive("ks0", kv.at[1 - c, pair_rows])
    block(0, True)

    for hop in range(4):
        around = (1, -1) if hop < 3 else (1,)
        for direction in around:
            got, used = kv_got(direction, hop), kv_used(direction, hop)

            @pl.when(got)
            def _():
                arrive(("kz", direction, hop), kv_at(c, -direction * (hop + 1)))

            if hop + 1 < (4 if direction > 0 else 3):
                kv_z(direction, hop + 1)

            @pl.when(used)
            def _():
                place = kv_at(c, -direction * (hop + 1))
                send(("ks", direction, hop), place, place, sibling, used)

        point()
        for direction in around:

            @pl.when(kv_used(direction, hop))
            def _():
                arrive(("ks", direction, hop), kv_at(1 - c, -direction * (hop + 1)))
                block(-direction * (hop + 1), False)

        point()

    mixed = acc[...] / l_run[...]
    for h in range(4):
        att[:, h * HD : (h + 1) * HD] = mixed[:, h * HD : (h + 1) * HD].T.astype(BF)
    locals_["op"].wait()

    @pl.loop(0, 4)
    def _(n):
        cols = pl.ds(pl.multiple_of(n * 512, 512), 512)
        share = jnp.dot(att[...], op[:, cols], preferred_element_type=F32).astype(BF)
        for owner in range(8):
            part[owner % 2, owner // 2, :, cols] = share[owner * 16 : owner * 16 + 16]

    send("hs", part.at[1 - c], part_in, sibling)
    point()

    for name in ("ids", "probs", "resid", "gain"):
        locals_[name].wait()
    turn[...] = jnp.zeros_like(turn)
    turn[0, :8, :16] = ids[...].astype(F32)
    turn[1, :8, :16] = probs[...]
    ids_of = turn[0].T
    probs_of = turn[1].T
    lane = lax.broadcasted_iota(jnp.int32, (16, 128), 1)
    low = lax.rem(lane, 16).astype(F32)
    chosen = jnp.zeros((16, 128), F32)
    weight = jnp.zeros((16, 128), F32)
    for k in range(8):
        hit = ids_of[:16, k : k + 1] == low
        chosen = jnp.where(hit, 1.0, chosen)
        weight = jnp.where(hit, probs_of[:16, k : k + 1], weight)
    before = (
        lax.broadcasted_iota(jnp.int32, (16, 16), 1) < lax.broadcasted_iota(jnp.int32, (16, 16), 0)
    ).astype(BF)
    rank = jnp.dot(before, chosen.astype(BF), preferred_element_type=F32)
    weight = jnp.where(rank < CAP - 0.5, weight, 0.0)
    high = weight.astype(BF).astype(F32)
    middle = (weight - high).astype(BF).astype(F32)
    least = weight - high - middle
    coded = jnp.where(
        lane < 16, high, jnp.where(lane < 32, middle, jnp.where(lane < 48, least, 0.0))
    )
    rows[0, e, :, D:] = coded.astype(BF)

    arrive("hs", part_in)
    part_sum[...] = (part[c].astype(F32) + part_in[...].astype(F32)).astype(BF)
    for dx in (2, 1, 3):
        send(("hx", dx), part_sum.at[lax.rem(x + dx, NX)], head_in.at[dx - 1], xdev(dx))
    point()
    mid = resid[...].astype(F32) + part_sum[x].astype(F32)
    for dx in (1, 3, 2):
        if dx == 2:
            point()
        arrive(("hx", dx), head_in.at[dx - 1])
        mid = mid + head_in[dx - 1].astype(F32)
    mid_ref[...] = mid
    mean = jnp.mean(mid * mid, axis=1, keepdims=True)
    rows[0, e, :, :D] = (mid * lax.rsqrt(mean + 1e-06) * gain[...]).astype(BF)

    own = rows.at[0, e]
    send("ap", own, rows.at[1, e], partner)
    for dx in (2, 1, 3):
        send(("ax", 0, dx), own, own, xdev(dx))
    send(("as", 0, 0), own, own, sibling)
    point()
    other = rows.at[1, e]
    arrive("ap", other)
    for dx in (2, 1, 3):
        send(("ax", 1, dx), other, other, xdev(dx))
    send(("as", 1, 0), other, other, sibling)
    point()
    for r in range(2):
        for dx in (1, 3, 2):
            come = rows.at[r, lax.rem(x - dx + NX, NX) * 2 + c]
            arrive(("ax", r, dx), come)
            send(("as", r, dx), come, come, sibling)
        point()
    for r in range(2):
        for dx in range(4):
            arrive(("as", r, dx), rows.at[r, lax.rem(x - dx + NX, NX) * 2 + 1 - c])
    while len(events) > 2:
        events.pop(0)()
    for p in range(3):
        locals_[("w", p)].wait()
    for dz in range(1, NZ):
        arrive(("wy", 1, dz), up_at(shard(dz, 1)))
    arrive(("wy", 1, 0), up_at(shard(0, 1)))
    upped[...] = jnp.dot(rows[:, :, :, :D].reshape(256, D), up_w[...], preferred_element_type=F32)
    while events:
        events.pop(0)()
    codes = rows[:, :, :, D:].reshape(256, 128).astype(F32)
    lanes = lax.broadcasted_iota(jnp.int32, (256, 128), 1)
    mine = (lax.rem(lanes, 16) == e * 2 + role) & (lanes < 48)
    coef = jnp.sum(jnp.where(mine, codes, 0.0), axis=1, keepdims=True)
    for r in (1, 0):
        tokens = rows[r, :, :, :D].reshape(128, D)
        gated = jnp.dot(tokens, gate_w[...], preferred_element_type=F32)
        of_row = pl.ds(r * 128, 128)
        hid[of_row] = (gated / (1.0 + jnp.exp(-gated)) * upped[of_row]).astype(BF)
        if r == 1:
            for dz in range(NZ):
                arrive(("wy", 2, dz), down_at(shard(dz, 1)))

        @pl.loop(0, 4)
        def _(n):
            cols = pl.ds(pl.multiple_of(n * 512, 512), 512)
            own_hid = hid[r * 128 : r * 128 + 128]
            made = jnp.dot(own_hid, down_w[:, cols], preferred_element_type=F32)
            made = (made.astype(BF).astype(F32) * coef[r * 128 : r * 128 + 128]).astype(BF)
            for owner in range(8):
                moe[owner % 2, r, owner // 2, :, cols] = made[owner * 16 : owner * 16 + 16]

        send(("ms", r), moe.at[1 - c, r], moe_in.at[r], sibling)
    for r in (1, 0):
        arrive(("ms", r), moe_in.at[r])
        moe_sum[r] = (moe[c, r].astype(F32) + moe_in[r].astype(F32)).astype(BF)
        for dx in (2, 1, 3):
            send(
                ("mx", r, dx), moe_sum.at[r, lax.rem(x + dx, NX)], moe_x.at[r, dx - 1], xdev(dx)
            )
    total = moe_sum[1, x].astype(F32)
    for dx in (1, 3, 2):
        arrive(("mx", 1, dx), moe_x.at[1, dx - 1])
        total = total + moe_x[1, dx - 1].astype(F32)
    y_out[...] = total.astype(BF)
    send("my", y_out, y_in, partner)
    total = mid_ref[...] + moe_sum[0, x].astype(F32)
    for dx in (1, 3, 2):
        arrive(("mx", 0, dx), moe_x.at[0, dx - 1])
        total = total + moe_x[0, dx - 1].astype(F32)
    for copy in sent:
        copy.wait_send()
    for cond, n, length in sent_if:

        @pl.when(cond)
        def _():
            like = kv.at[0, pl.ds(0, length)]
            pltpu.make_async_remote_copy(
                src_ref=like,
                dst_ref=like,
                send_sem=send_sem.at[n],
                recv_sem=recv_sem.at[n],
                device_id=sibling,
                device_id_type=MESH,
            ).wait_send()

    arrive("my", y_in)
    out_ref[...] = (total + y_in[...].astype(F32)).astype(BF)
    assert len(keys) <= N_SEM


def on_device(
    queries, keys, values, resid, out_proj, norm_gain, expert_ids, gate_probs, w_gate, w_up, w_down
):
    in_hbm = pl.BlockSpec(memory_space=pltpu.HBM)
    return pl.pallas_call(
        layer_kernel,
        out_shape=jax.ShapeDtypeStruct((16, D), BF),
        in_specs=[in_hbm] * 11,
        out_specs=pl.BlockSpec(memory_space=pltpu.VMEM),
        scratch_shapes=[
            pltpu.VMEM((512, HD), BF),
            pltpu.VMEM((2, 2048, HD), BF),
            pltpu.VMEM((512, D), BF),
            pltpu.VMEM((16, D), BF),
            pltpu.VMEM((1, D), F32),
            pltpu.VMEM((8, 16), jnp.int32),
            pltpu.VMEM((8, 16), F32),
            pltpu.VMEM((2, 128, 128), F32),
            pltpu.VMEM((D, FF), BF),
            pltpu.VMEM((D, FF), BF),
            pltpu.VMEM((FF, D), BF),
            pltpu.VMEM((1, 512), F32),
            pltpu.VMEM((1, 512), F32),
            pltpu.VMEM((HD, 512), F32),
            pltpu.VMEM((128, 512), BF),
            pltpu.VMEM((2, 4, 16, D), BF),
            pltpu.VMEM((4, 16, D), BF),
            pltpu.VMEM((4, 16, D), BF),
            pltpu.VMEM((3, 16, D), BF),
            pltpu.VMEM((16, D), F32),
            pltpu.VMEM((2, 8, 16, MSG), BF),
            pltpu.VMEM((256, FF), BF),
            pltpu.VMEM((256, FF), F32),
            pltpu.VMEM((2, 2, 4, 16, D), BF),
            pltpu.VMEM((2, 4, 16, D), BF),
            pltpu.VMEM((2, 4, 16, D), BF),
            pltpu.VMEM((2, 3, 16, D), BF),
            pltpu.VMEM((16, D), BF),
            pltpu.VMEM((16, D), BF),
            pltpu.SemaphoreType.DMA((16,)),
            pltpu.SemaphoreType.DMA((N_SEM,)),
            pltpu.SemaphoreType.DMA((N_SEM,)),
        ],
        compiler_params=pltpu.CompilerParams(
            collective_id=0, has_side_effects=True, vmem_limit_bytes=58 << 20
        ),
        cost_estimate=pl.CostEstimate(
            flops=2_000_000_000, bytes_accessed=6_000_000, transcendentals=1_000_000
        ),
        name="layer",
    )(
        queries,
        keys,
        values,
        resid,
        out_proj,
        norm_gain.reshape(1, D),
        expert_ids.T,
        gate_probs.T,
        w_gate,
        w_up,
        w_down,
    )


def solution(mesh):
    placed = (
        P(("dp", "ctx"), "exp"),
        P(("dp", "ctx"), None),
        P(("dp", "ctx"), None),
        P(("dp", "ctx", "exp"), None),
        P("exp", None),
        P(),
        P(("dp", "ctx", "exp"), None),
        P(("dp", "ctx", "exp"), None),
        P("exp", "ctx", None),
        P("exp", "ctx", None),
        P("exp", None, "ctx"),
    )
    return jax.shard_map(
        on_device,
        mesh=mesh,
        in_specs=placed,
        out_specs=P(("dp", "ctx", "exp"), None),
        check_vma=False,
    )
```

```python
import functools

import jax
import jax.numpy as jnp
from jax import lax
from jax.experimental import pallas as pl
from jax.experimental.pallas import tpu as pltpu
from jax.sharding import PartitionSpec as P

MESH = pl.DeviceIdType.MESH
BF = jnp.bfloat16
F32 = jnp.float32
HD = 128
D = 2048
FF = 384
NZ = 8
NX = 4
CAP = 10
MSG = D + 128
N_SEM = 160
STEPS = (2, 1, 1, 1, 1, 1, 1, 1, 1, 1, 1, 2, 0, 2, 2, 2, 1)


def layer_kernel(
    q_hbm,
    k_hbm,
    v_hbm,
    resid_hbm,
    op_hbm,
    gain_hbm,
    ids_hbm,
    probs_hbm,
    wg_hbm,
    wu_hbm,
    wd_hbm,
    out_ref,
    q4,
    kv,
    op,
    resid,
    gain,
    ids,
    probs,
    turn,
    gate_w,
    up_w,
    down_w,
    m_run,
    l_run,
    acc,
    att,
    part,
    part_in,
    part_sum,
    head_in,
    mid_ref,
    rows,
    hid,
    upped,
    moe,
    moe_in,
    moe_sum,
    moe_x,
    y_out,
    y_in,
    local_sem,
    send_sem,
    recv_sem,
):
    d = lax.axis_index("dp")
    i = lax.axis_index("ctx")
    e = lax.axis_index("exp")
    z, yl = lax.div(i, 2), lax.rem(i, 2)
    x, c = lax.div(e, 2), lax.rem(e, 2)
    role = lax.rem(d, 2)
    y = d * 2 + yl
    y_partner = lax.rem(y + 2 * yl - 1 + 8, 8)

    def zdev(dz):
        return (d, lax.rem(z + dz + NZ, NZ) * 2 + yl, e)

    def xdev(dx):
        return (d, i, lax.rem(x + dx, NX) * 2 + c)

    sibling = (d, i, x * 2 + 1 - c)
    pair = (d, z * 2 + 1 - yl, e)
    partner = (lax.div(y_partner, 2), z * 2 + lax.rem(y_partner, 2), e)

    keys = {}
    sent = []
    sent_if = []
    locals_ = {}

    def slot(key):
        return keys.setdefault(key, len(keys))

    def send(key, src, dst, device, cond=None):
        n = slot(key)
        copy = pltpu.make_async_remote_copy(
            src_ref=src,
            dst_ref=dst,
            send_sem=send_sem.at[n],
            recv_sem=recv_sem.at[n],
            device_id=device,
            device_id_type=MESH,
        )
        copy.start()
        if cond is None:
            sent.append(copy)
        else:
            sent_if.append((cond, n, src.shape[0]))

    def arrive(key, dst):
        n = slot(key)
        pltpu.make_async_remote_copy(
            src_ref=dst,
            dst_ref=dst,
            send_sem=send_sem.at[n],
            recv_sem=recv_sem.at[n],
            device_id=sibling,
            device_id_type=MESH,
        ).wait_recv()

    def load(key, src, dst):
        copy = pltpu.make_async_copy(src, dst, local_sem.at[len(locals_)])
        copy.start()
        locals_[key] = copy

    def mod_z(dz):
        return lax.rem(z + dz + NZ, NZ)

    own_rows = pl.ds(pl.multiple_of(i * 128, 128), 128)
    head_cols = pl.ds(pl.multiple_of(x * HD, HD), HD)
    load("k", k_hbm.at[:, head_cols], kv.at[0, own_rows])
    load("v", v_hbm.at[:, head_cols], kv.at[1, own_rows])
    for h in range(4):
        load(("q", h), q_hbm.at[:, pl.ds(h * HD, HD)], q4.at[pl.ds(h * HD, HD)])
    load("op", op_hbm, op)
    load("resid", resid_hbm, resid)
    load("gain", gain_hbm, gain)
    load("ids", ids_hbm, ids)
    load("probs", probs_hbm, probs)

    def gate_at(s):
        return gate_w.at[pl.ds(pl.multiple_of(s * 128, 128), 128)]

    def up_at(s):
        return up_w.at[pl.ds(pl.multiple_of(s * 128, 128), 128)]

    def down_at(s):
        return down_w.at[:, pl.ds(pl.multiple_of(s * 128, 128), 128)]

    places = (gate_at, up_at, down_at)
    firsts = (wg_hbm.at[role], wu_hbm.at[role], wd_hbm.at[role])
    others = (wg_hbm.at[1 - role], wu_hbm.at[1 - role], wd_hbm.at[1 - role])
    for p in range(3):
        load(("w", p), firsts[p], places[p](i))

    barrier = pltpu.get_barrier_semaphore()
    near = [zdev(1), zdev(-1), pair, partner, sibling, xdev(1), xdev(2), xdev(3)]
    for device in near:
        pl.semaphore_signal(barrier, inc=1, device_id=device, device_id_type=MESH)
    pl.semaphore_wait(barrier, len(near))

    def hops(p, w, direction):
        return 4 if ((p + w) % 2 == 0) == (direction > 0) else 3

    def shard(dz, w):
        return mod_z(dz) * 2 + (yl if w == 0 else 1 - yl)

    def weight_z(p, w, direction, hop):
        place = places[p](shard(-direction * hop, w))
        src = firsts[p] if (w == 0 and hop == 0) else place
        send(("wz", p, w, direction, hop), src, place, zdev(direction))

    def weight_y(p, dz):
        place = places[p](shard(dz, 0))
        if dz == 0:
            send(("wy", p, 0), others[p], place, partner)
        else:
            send(("wy", p, dz % NZ), place, place, pair)

    def weight_step(p, w, direction, hop):
        place = places[p](shard(-direction * (hop + 1), w))
        arrive(("wz", p, w, direction, hop), place)
        if hop + 1 < hops(p, w, direction):
            weight_z(p, w, direction, hop + 1)
        if p > 0:
            weight_y(p, -direction * (hop + 1))

    def weight_start(p, w):
        if w == 1:
            arrive(("wy", p, 0), places[p](shard(0, 1)))
        for direction in (1, -1):
            weight_z(p, w, direction, 0)

    def weight_hop(p, w, hop):
        for direction in (1, -1):
            if hop < hops(p, w, direction):
                weight_step(p, w, direction, hop)

    streams = ((1, 0), (2, 0), (0, 0), (0, 1))
    events = [functools.partial(weight_start, p, w) for p, w in streams]
    for hop in range(4):
        events += [functools.partial(weight_hop, p, w, hop) for p, w in streams]
    points = list(STEPS)

    def point():
        for _ in range(points.pop(0) if points else len(events)):
            if events:
                events.pop(0)()

    def kv_at(kind, dz):
        return kv.at[kind, pl.ds(pl.multiple_of(mod_z(dz) * 256, 256), 256)]

    pair_rows = pl.ds(pl.multiple_of((z * 2 + 1 - yl) * 128, 128), 128)

    def kv_got(direction, hop):
        if direction > 0:
            return z >= hop + 1
        return ((z == 7) | (z <= 1), (z >= 6) | (z == 0), z >= 5)[hop]

    def kv_used(direction, hop):
        return z >= hop + 1 if direction > 0 else z + hop + 1 >= NZ

    def kv_more(direction, hop):
        if hop == 0:
            return z <= NZ - 2 if direction > 0 else z <= 2
        got = kv_got(direction, hop - 1)
        return got & (z <= NZ - 2) if direction > 0 else got

    def kv_z(direction, hop):
        more = kv_more(direction, hop)

        @pl.when(more)
        def _():
            place = kv_at(c, -direction * hop)
            send(("kz", direction, hop), place, place, zdev(direction), more)

    locals_["k"].wait()
    locals_["v"].wait()
    send("kp", kv.at[c, own_rows], kv.at[c, own_rows], pair)
    for p in range(3):
        weight_y(p, 0)
    point()

    arrive("kp", kv.at[c, pair_rows])
    for direction in (1, -1):
        kv_z(direction, 0)
    send("ks0", kv.at[c, pair_rows], kv.at[c, pair_rows], sibling)
    point()

    def block(dz, first):
        key_rows = pl.ds(pl.multiple_of(mod_z(dz) * 256, 256), 256)
        scores = lax.dot_general(
            kv[0, key_rows, :], q4[...], (((1,), (1,)), ((), ())), preferred_element_type=F32
        ) * (float(HD) ** -0.5)
        if first:
            key_pos = z * 256 + lax.broadcasted_iota(jnp.int32, (256, 512), 0)
            query_pos = i * 128 + lax.rem(lax.broadcasted_iota(jnp.int32, (256, 512), 1), 128)
            scores = jnp.where(key_pos <= query_pos, scores, -1e30)
        peak = jnp.max(scores, axis=0, keepdims=True)
        if not first:
            old = m_run[...]
            peak = jnp.maximum(peak, old)
        raw = jnp.exp(scores - peak)
        total = jnp.sum(raw, axis=0, keepdims=True)
        mixed = lax.dot_general(
            kv[1, key_rows, :],
            raw.astype(BF),
            (((0,), (0,)), ((), ())),
            preferred_element_type=F32,
        )
        m_run[...] = peak
        if first:
            l_run[...] = total
            acc[...] = mixed
        else:
            factor = jnp.exp(old - peak)
            l_run[...] = l_run[...] * factor + total
            acc[...] = acc[...] * factor + mixed

    for h in range(4):
        locals_[("q", h)].wait()
    arrive("ks0", kv.at[1 - c, pair_rows])
    block(0, True)

    for hop in range(4):
        around = (1, -1) if hop < 3 else (1,)
        for direction in around:
            got, used = kv_got(direction, hop), kv_used(direction, hop)

            @pl.when(got)
            def _():
                arrive(("kz", direction, hop), kv_at(c, -direction * (hop + 1)))

            if hop + 1 < (4 if direction > 0 else 3):
                kv_z(direction, hop + 1)

            @pl.when(used)
            def _():
                place = kv_at(c, -direction * (hop + 1))
                send(("ks", direction, hop), place, place, sibling, used)

        point()
        for direction in around:

            @pl.when(kv_used(direction, hop))
            def _():
                arrive(("ks", direction, hop), kv_at(1 - c, -direction * (hop + 1)))
                block(-direction * (hop + 1), False)

        point()

    mixed = acc[...] / l_run[...]
    for h in range(4):
        att[:, h * HD : (h + 1) * HD] = mixed[:, h * HD : (h + 1) * HD].T.astype(BF)
    locals_["op"].wait()

    @pl.loop(0, 4)
    def _(n):
        cols = pl.ds(pl.multiple_of(n * 512, 512), 512)
        share = jnp.dot(att[...], op[:, cols], preferred_element_type=F32).astype(BF)
        for owner in range(8):
            part[owner % 2, owner // 2, :, cols] = share[owner * 16 : owner * 16 + 16]

    send("hs", part.at[1 - c], part_in, sibling)
    point()

    for name in ("ids", "probs", "resid", "gain"):
        locals_[name].wait()
    turn[...] = jnp.zeros_like(turn)
    turn[0, :8, :16] = ids[...].astype(F32)
    turn[1, :8, :16] = probs[...]
    ids_of = turn[0].T
    probs_of = turn[1].T
    lane = lax.broadcasted_iota(jnp.int32, (16, 128), 1)
    low = lax.rem(lane, 16).astype(F32)
    chosen = jnp.zeros((16, 128), F32)
    weight = jnp.zeros((16, 128), F32)
    for k in range(8):
        hit = ids_of[:16, k : k + 1] == low
        chosen = jnp.where(hit, 1.0, chosen)
        weight = jnp.where(hit, probs_of[:16, k : k + 1], weight)
    before = (
        lax.broadcasted_iota(jnp.int32, (16, 16), 1) < lax.broadcasted_iota(jnp.int32, (16, 16), 0)
    ).astype(BF)
    rank = jnp.dot(before, chosen.astype(BF), preferred_element_type=F32)
    weight = jnp.where(rank < CAP - 0.5, weight, 0.0)
    high = weight.astype(BF).astype(F32)
    middle = (weight - high).astype(BF).astype(F32)
    least = weight - high - middle
    coded = jnp.where(
        lane < 16, high, jnp.where(lane < 32, middle, jnp.where(lane < 48, least, 0.0))
    )
    rows[0, e, :, D:] = coded.astype(BF)

    arrive("hs", part_in)
    part_sum[...] = (part[c].astype(F32) + part_in[...].astype(F32)).astype(BF)
    for dx in (2, 1, 3):
        send(("hx", dx), part_sum.at[lax.rem(x + dx, NX)], head_in.at[dx - 1], xdev(dx))
    point()
    mid = resid[...].astype(F32) + part_sum[x].astype(F32)
    for dx in (1, 3, 2):
        if dx == 2:
            point()
        arrive(("hx", dx), head_in.at[dx - 1])
        mid = mid + head_in[dx - 1].astype(F32)
    mid_ref[...] = mid
    mean = jnp.mean(mid * mid, axis=1, keepdims=True)
    rows[0, e, :, :D] = (mid * lax.rsqrt(mean + 1e-06) * gain[...]).astype(BF)

    own = rows.at[0, e]
    send("ap", own, rows.at[1, e], partner)
    for dx in (2, 1, 3):
        send(("ax", 0, dx), own, own, xdev(dx))
    send(("as", 0, 0), own, own, sibling)
    point()
    other = rows.at[1, e]
    arrive("ap", other)
    for dx in (2, 1, 3):
        send(("ax", 1, dx), other, other, xdev(dx))
    send(("as", 1, 0), other, other, sibling)
    point()
    for r in range(2):
        for dx in (1, 3, 2):
            come = rows.at[r, lax.rem(x - dx + NX, NX) * 2 + c]
            arrive(("ax", r, dx), come)
            send(("as", r, dx), come, come, sibling)
        point()
    for r in range(2):
        for dx in range(4):
            arrive(("as", r, dx), rows.at[r, lax.rem(x - dx + NX, NX) * 2 + 1 - c])
    while len(events) > 2:
        events.pop(0)()
    for p in range(3):
        locals_[("w", p)].wait()
    for dz in range(1, NZ):
        arrive(("wy", 1, dz), up_at(shard(dz, 1)))
    arrive(("wy", 1, 0), up_at(shard(0, 1)))
    upped[...] = jnp.dot(rows[:, :, :, :D].reshape(256, D), up_w[...], preferred_element_type=F32)
    while events:
        events.pop(0)()
    codes = rows[:, :, :, D:].reshape(256, 128).astype(F32)
    lanes = lax.broadcasted_iota(jnp.int32, (256, 128), 1)
    mine = (lax.rem(lanes, 16) == e * 2 + role) & (lanes < 48)
    coef = jnp.sum(jnp.where(mine, codes, 0.0), axis=1, keepdims=True)
    for r in (1, 0):
        tokens = rows[r, :, :, :D].reshape(128, D)
        gated = jnp.dot(tokens, gate_w[...], preferred_element_type=F32)
        of_row = pl.ds(r * 128, 128)
        hid[of_row] = (gated / (1.0 + jnp.exp(-gated)) * upped[of_row]).astype(BF)
        if r == 1:
            for dz in range(NZ):
                arrive(("wy", 2, dz), down_at(shard(dz, 1)))

        @pl.loop(0, 4)
        def _(n):
            cols = pl.ds(pl.multiple_of(n * 512, 512), 512)
            own_hid = hid[r * 128 : r * 128 + 128]
            made = jnp.dot(own_hid, down_w[:, cols], preferred_element_type=F32)
            made = (made.astype(BF).astype(F32) * coef[r * 128 : r * 128 + 128]).astype(BF)
            for owner in range(8):
                moe[owner % 2, r, owner // 2, :, cols] = made[owner * 16 : owner * 16 + 16]

        send(("ms", r), moe.at[1 - c, r], moe_in.at[r], sibling)
    earlier = len(sent)
    for r in (1, 0):
        arrive(("ms", r), moe_in.at[r])
        moe_sum[r] = (moe[c, r].astype(F32) + moe_in[r].astype(F32)).astype(BF)
        for dx in (2, 1, 3):
            send(
                ("mx", r, dx), moe_sum.at[r, lax.rem(x + dx, NX)], moe_x.at[r, dx - 1], xdev(dx)
            )
    for copy in sent[:earlier]:
        copy.wait_send()
    del sent[:earlier]
    for cond, n, length in sent_if:

        @pl.when(cond)
        def _():
            like = kv.at[0, pl.ds(0, length)]
            pltpu.make_async_remote_copy(
                src_ref=like,
                dst_ref=like,
                send_sem=send_sem.at[n],
                recv_sem=recv_sem.at[n],
                device_id=sibling,
                device_id_type=MESH,
            ).wait_send()

    total = moe_sum[1, x].astype(F32)
    for dx in (1, 3, 2):
        arrive(("mx", 1, dx), moe_x.at[1, dx - 1])
        total = total + moe_x[1, dx - 1].astype(F32)
    y_out[...] = total.astype(BF)
    send("my", y_out, y_in, partner)
    total = mid_ref[...] + moe_sum[0, x].astype(F32)
    for dx in (1, 3, 2):
        arrive(("mx", 0, dx), moe_x.at[0, dx - 1])
        total = total + moe_x[0, dx - 1].astype(F32)
    for copy in sent:
        copy.wait_send()
    arrive("my", y_in)
    out_ref[...] = (total + y_in[...].astype(F32)).astype(BF)
    assert len(keys) <= N_SEM


def on_device(
    queries, keys, values, resid, out_proj, norm_gain, expert_ids, gate_probs, w_gate, w_up, w_down
):
    in_hbm = pl.BlockSpec(memory_space=pltpu.HBM)
    return pl.pallas_call(
        layer_kernel,
        out_shape=jax.ShapeDtypeStruct((16, D), BF),
        in_specs=[in_hbm] * 11,
        out_specs=pl.BlockSpec(memory_space=pltpu.VMEM),
        scratch_shapes=[
            pltpu.VMEM((512, HD), BF),
            pltpu.VMEM((2, 2048, HD), BF),
            pltpu.VMEM((512, D), BF),
            pltpu.VMEM((16, D), BF),
            pltpu.VMEM((1, D), F32),
            pltpu.VMEM((8, 16), jnp.int32),
            pltpu.VMEM((8, 16), F32),
            pltpu.VMEM((2, 128, 128), F32),
            pltpu.VMEM((D, FF), BF),
            pltpu.VMEM((D, FF), BF),
            pltpu.VMEM((FF, D), BF),
            pltpu.VMEM((1, 512), F32),
            pltpu.VMEM((1, 512), F32),
            pltpu.VMEM((HD, 512), F32),
            pltpu.VMEM((128, 512), BF),
            pltpu.VMEM((2, 4, 16, D), BF),
            pltpu.VMEM((4, 16, D), BF),
            pltpu.VMEM((4, 16, D), BF),
            pltpu.VMEM((3, 16, D), BF),
            pltpu.VMEM((16, D), F32),
            pltpu.VMEM((2, 8, 16, MSG), BF),
            pltpu.VMEM((256, FF), BF),
            pltpu.VMEM((256, FF), F32),
            pltpu.VMEM((2, 2, 4, 16, D), BF),
            pltpu.VMEM((2, 4, 16, D), BF),
            pltpu.VMEM((2, 4, 16, D), BF),
            pltpu.VMEM((2, 3, 16, D), BF),
            pltpu.VMEM((16, D), BF),
            pltpu.VMEM((16, D), BF),
            pltpu.SemaphoreType.DMA((16,)),
            pltpu.SemaphoreType.DMA((N_SEM,)),
            pltpu.SemaphoreType.DMA((N_SEM,)),
        ],
        compiler_params=pltpu.CompilerParams(
            collective_id=0, has_side_effects=True, vmem_limit_bytes=58 << 20
        ),
        cost_estimate=pl.CostEstimate(
            flops=2_000_000_000, bytes_accessed=6_000_000, transcendentals=1_000_000
        ),
        name="layer",
    )(
        queries,
        keys,
        values,
        resid,
        out_proj,
        norm_gain.reshape(1, D),
        expert_ids.T,
        gate_probs.T,
        w_gate,
        w_up,
        w_down,
    )


def solution(mesh):
    placed = (
        P(("dp", "ctx"), "exp"),
        P(("dp", "ctx"), None),
        P(("dp", "ctx"), None),
        P(("dp", "ctx", "exp"), None),
        P("exp", None),
        P(),
        P(("dp", "ctx", "exp"), None),
        P(("dp", "ctx", "exp"), None),
        P("exp", "ctx", None),
        P("exp", "ctx", None),
        P("exp", None, "ctx"),
    )
    return jax.shard_map(
        on_device,
        mesh=mesh,
        in_specs=placed,
        out_specs=P(("dp", "ctx", "exp"), None),
        check_vma=False,
    )
```
